256 devices in a mesh: dp: 256 (over x, y, z, core).
Axes of the slice: x: 4, y: 4, z: 8, core: 2. Of those that a mesh axis runs over, the one named last changes fastest.
Arguments:
- image_embed: bfloat16 [131072, 1152], P('dp'), may hold values from -0.1796875 to 0.1796875
- text_embed: bfloat16 [131072, 1152], P('dp'), may hold values from -0.1796875 to 0.1796875
- logit_scale: float32 [1], replicated, may hold values from 4 to 16
- logit_bias: float32 [1], replicated, may hold values from -3 to -1
Outputs:
- row_loss: float32 [131072], P('dp')
- image_grad: float32 [131072, 1152], P('dp')
- text_grad: float32 [131072, 1152], P('dp')
The draws below stay inside these ranges and needn't reach their ends.
All inputs are finite; a program needn't handle non-finite values.
Results may differ from the reference program's by a relative error of at most 0.0046.
Values may be sent and summed in bfloat16 or wider, within the bound.
A program may use at most 64 MiB of HBM per device.

```python
import math
import jax
import jax.numpy as jnp
from jax import lax

D = 1152
ROWS = 512
REACH = 2
WINDOW = 5
BATCH = 131072
N_DP = 256


def block_scale(stream_key, shape, split, least, largest):
    def one(position, blocks):
        draws = jax.random.uniform(jax.random.fold_in(jax.random.fold_in(stream_key, 6), position), (blocks,), jnp.float32, least / len(split), largest / len(split))
        return jnp.repeat(jnp.exp(draws), shape[position] // blocks).reshape((-1,) + (1,) * (len(shape) - position - 1))

    level = one(*split[0])
    for cut in split[1:]:
        level = level * one(*cut)
    return level


def normal_values(rng, shape, deviation, bound, split=(), held_as=jnp.bfloat16):
    drawn = jax.random.normal(rng, shape, jnp.float32) * deviation
    if len(split) > 0:
        drawn = block_scale(rng, shape, split, -0.22, 0.18) * drawn
    return jnp.clip(drawn, min=-bound, max=bound).astype(held_as)


def setup_inputs(seed: int = 0) -> dict:
    arg_keys = jax.random.split(jax.random.key(seed), 5)
    return {
        "image_embed": normal_values(arg_keys[0], (BATCH, D), 0.03, 0.1796875, ((0, 256),)),
        "text_embed": normal_values(arg_keys[1], (BATCH, D), 0.03, 0.1796875, ((0, 256),)),
        "logit_scale": jnp.clip(jnp.exp(jax.random.uniform(arg_keys[2], (1,), jnp.float32, math.log(4.0), math.log(16.0))), 4.0, 16.0),
        "logit_bias": jnp.clip(jax.random.uniform(arg_keys[3], (1,), jnp.float32, -3.0, -1.0), -3.0, -1.0),
    }


eps_norm = 1e-06

def unit_rows(raw_rows):
    values = raw_rows.astype(jnp.float32)
    length = jnp.sqrt(lax.optimization_barrier(jnp.sum(values * values, axis=1, keepdims=True)) + eps_norm)
    return (values / length, length)

def unit_grad(grad_unit, unit_values, length):
    along_unit = lax.optimization_barrier(jnp.sum(grad_unit * unit_values, axis=1, keepdims=True))
    return (grad_unit - unit_values * along_unit) / length

def pair_block(image_rows, text_rows, scale_value, bias_value, positive):
    cosine = lax.dot_general(image_rows, text_rows, (((1,), (1,)), ((), ())), preferred_element_type=jnp.float32)
    logits = scale_value * cosine + bias_value
    if positive:
        target = jnp.eye(logits.shape[0], dtype=logits.dtype)
    else:
        target = jnp.zeros_like(logits)
    pair_loss = jax.nn.softplus(logits) - target * logits
    weights = (scale_value * (jax.nn.sigmoid(logits) - target)).astype(jnp.bfloat16)
    return (lax.optimization_barrier(jnp.sum(pair_loss, axis=1)), weights)

def reference(image_embed, text_embed, logit_scale, logit_bias):
    scale_value = logit_scale[0]
    bias_value = logit_bias[0]
    image_unit, image_length = unit_rows(image_embed)
    text_unit, text_length = unit_rows(text_embed)
    image_rows = image_unit.astype(jnp.bfloat16)
    text_rows = text_unit.astype(jnp.bfloat16)

    def one_block(text_total, block_index):
        image_start = (block_index * ROWS).astype(jnp.int32)
        image_block = lax.dynamic_slice_in_dim(image_rows, image_start, ROWS, 0)
        loss_sum = jnp.zeros((ROWS,), jnp.float32)
        grad_unit = jnp.zeros((ROWS, D), jnp.float32)
        for offset in range(-REACH, REACH + 1):
            other_block = (block_index + offset) % N_DP
            start_row = (other_block * ROWS).astype(jnp.int32)
            text_block = lax.dynamic_slice_in_dim(text_rows, start_row, ROWS, 0)
            row_sum, weights = pair_block(image_block, text_block, scale_value, bias_value, offset == 0)
            loss_sum = loss_sum + row_sum
            grad_unit = grad_unit + jnp.dot(weights, text_block, preferred_element_type=jnp.float32)
            partial_text = lax.dot_general(weights, image_block, (((0,), (0,)), ((), ())), preferred_element_type=jnp.float32)
            held_rows = lax.dynamic_slice_in_dim(text_total, start_row, ROWS, 0)
            text_total = lax.dynamic_update_slice_in_dim(text_total, held_rows + partial_text, start_row, 0)
        return (text_total, (loss_sum / (WINDOW * ROWS), grad_unit))
    text_total, (loss_blocks, image_blocks) = lax.scan(one_block, jnp.zeros((BATCH, D), jnp.float32), jnp.arange(N_DP, dtype=jnp.int32))
    row_loss = loss_blocks.reshape(BATCH)
    image_total = image_blocks.reshape(BATCH, D)
    image_grad = unit_grad(image_total, image_unit, image_length)
    text_grad = unit_grad(text_total, text_unit, text_length)
    return (row_loss, image_grad, text_grad)
```

```python
import functools

import jax
import jax.numpy as jnp
from jax import lax
from jax.experimental import pallas as pl
from jax.experimental.pallas import tpu as pltpu
from jax.sharding import PartitionSpec as P

MESH = pl.DeviceIdType.MESH
REACH = 2
WINDOW = 5
EPS = 1e-06
UP, DOWN, RELAY, SIBLING, OWN = range(5)
ROUNDS = 4


def inverse_length(rows):
    return lax.rsqrt(jnp.sum(rows * rows, axis=1, keepdims=True) + EPS)


def exchange(n, img, txt, scale_ref, bias_ref, image_grad, text_grad, loss_out,
             buf, own, chunk, total, inverse, loss_acc, load_sem, send_sem, recv_sem):
    rows = img.shape[0]
    part = rows // 2
    me = lax.axis_index("dp")
    core = lax.rem(me, 2)
    sibling = me + 1 - 2 * core
    upper = lax.rem(me + 2, n)
    lower = lax.rem(me + n - 2, n)
    relayed = 1 - core

    barrier = pltpu.get_barrier_semaphore()
    for other in (upper, lower, sibling):
        pl.semaphore_signal(barrier, inc=1, device_id=(other,), device_id_type=MESH)
    loads = [pltpu.make_async_copy(source, buf.at[OWN, kind], load_sem.at[kind]) for kind, source in enumerate((txt, img))]
    for load in loads:
        load.start()
    pl.semaphore_wait(barrier, 3)

    def place(step):
        return step // 2, pl.ds(pl.multiple_of(lax.rem(step, 2) * part, part), part)

    def outgoing(source, target, way, step):
        kind, span = step // 2, pl.ds((step % 2) * part, part)
        return pltpu.make_async_remote_copy(
            source[kind].at[span], buf.at[way, kind, span], send_sem.at[way, step], recv_sem.at[way, step],
            device_id=(target,), device_id_type=MESH,
        )

    def relay(step):
        kind, span = place(step)
        return pltpu.make_async_remote_copy(
            buf.at[relayed, kind, span], buf.at[RELAY, kind, span], send_sem.at[RELAY, step], recv_sem.at[RELAY, step],
            device_id=(sibling,), device_id_type=MESH,
        )

    def arrived(way, step):
        kind, span = place(step)
        return pltpu.make_async_remote_copy(
            buf.at[way, kind, span], buf.at[way, kind, span], send_sem.at[way, step], recv_sem.at[way, step],
            device_id=(sibling,), device_id_type=MESH,
        )

    sends = []
    for step in range(ROUNDS):
        for way, target in ((UP, upper), (DOWN, lower)):
            sends.append(outgoing((txt, img), target, way, step))
    for step in range(ROUNDS):
        sends.append(outgoing((txt, img), sibling, SIBLING, step))
    for send in sends:
        send.start()

    scale = scale_ref[0]
    bias = bias_ref[0]
    for load in loads:
        load.wait()
    total[...] = jnp.zeros_like(total)
    loss_acc[...] = jnp.zeros_like(loss_acc)

    @pl.loop(0, 2)
    def _(kind):
        @pl.loop(0, rows // 128)
        def _(tile):
            span = pl.ds(pl.multiple_of(tile * 128, 128), 128)
            values = buf[OWN, 1 - kind, span].astype(jnp.float32)
            factor = inverse_length(values)
            inverse[kind, span] = factor
            own[kind, span] = (values * factor).astype(jnp.bfloat16)

    def pairs(way, step, is_own):
        kind, span = place(step)

        for tile in range(part // 128):
            rows_here = pl.ds(pl.multiple_of(lax.rem(step, 2) * part + tile * 128, 128), 128)
            values = buf[way, kind, rows_here].astype(jnp.float32)
            chunk[tile * 128:(tile + 1) * 128] = (values * inverse_length(values)).astype(jnp.bfloat16)
        offset = jnp.where(is_own, lax.rem(step, 2) * part, -2 * rows)
        for tile in range(rows // 256):
            held = pl.ds(tile * 256, 256)
            cosine = lax.dot_general(own[kind, held], chunk[...], (((1,), (1,)), ((), ())), preferred_element_type=jnp.float32)
            logits = scale * cosine + bias
            row = lax.broadcasted_iota(jnp.int32, logits.shape, 0) + tile * 256
            column = lax.broadcasted_iota(jnp.int32, logits.shape, 1)
            positive = row - column == offset
            grown = jnp.exp(logits)
            above = 1.0 + grown
            small = grown * (1.0 - grown * (0.5 - grown * (1.0 / 3.0)))
            loss = jnp.where(grown < 0.0078125, small, jnp.log(above)) - jnp.where(positive, logits, 0.0)
            loss_acc[kind, held] += functools.reduce(jnp.add, [loss[:, i:i + 128] for i in range(0, part, 128)])
            weights = (scale * (grown * pl.reciprocal(above) - jnp.where(positive, 1.0, 0.0))).astype(jnp.bfloat16)
            total[kind, held] += jnp.dot(weights, chunk[...], preferred_element_type=jnp.float32)

    @pl.loop(0, ROUNDS)
    def _(step):
        pairs(OWN, step, True)

    @pl.loop(0, ROUNDS)
    def _(step):
        arrived(SIBLING, step).wait_recv()
        pairs(SIBLING, step, False)

    def finish(kind, out):
        @pl.loop(0, rows // 64)
        def _(tile):
            span = pl.ds(pl.multiple_of(tile * 64, 64), 64)
            factor = inverse[kind, span]
            unit = buf[OWN, 1 - kind, span].astype(jnp.float32) * factor
            summed = total[kind, span]
            along = jnp.sum(summed * unit, axis=1, keepdims=True)
            out[span] = (summed - unit * along) * factor

    @pl.loop(0, ROUNDS * 3)
    def _(turn):
        step, order = turn // 3, lax.rem(turn, 3)
        way = jnp.where(order == 0, relayed, jnp.where(order == 1, 1 - relayed, RELAY))
        arrived(way, step).wait_recv()

        @pl.when(order == 0)
        def _():
            relay(step).start()

        pairs(way, step, False)

        @pl.when(turn == 5)
        def _():
            finish(0, image_grad)

    finish(1, text_grad)
    ones = jnp.full((8, 128), 1.0, jnp.float32)
    row_loss = lax.dot_general(
        ones, loss_acc[0], (((1,), (1,)), ((), ())), preferred_element_type=jnp.float32, precision=lax.Precision.HIGHEST
    )
    loss_out[...] = row_loss * (1.0 / (WINDOW * rows))
    for send in sends:
        send.wait_send()
    for step in range(ROUNDS):
        relay(step).wait_send()


def local(n, image_embed, text_embed, logit_scale, logit_bias):
    rows, width = image_embed.shape
    image_grad, text_grad, loss = pl.pallas_call(
        functools.partial(exchange, n),
        out_shape=(
            pltpu.VMEM((rows, width), jnp.float32),
            pltpu.VMEM((rows, width), jnp.float32),
            pltpu.VMEM((8, rows), jnp.float32),
        ),
        in_specs=[
            pl.BlockSpec(memory_space=pl.ANY),
            pl.BlockSpec(memory_space=pl.ANY),
            pl.BlockSpec(memory_space=pltpu.SMEM),
            pl.BlockSpec(memory_space=pltpu.SMEM),
        ],
        out_specs=[pl.BlockSpec(memory_space=pltpu.VMEM)] * 3,
        scratch_shapes=[
            pltpu.VMEM((5, 2, rows, width), jnp.bfloat16),
            pltpu.VMEM((2, rows, width), jnp.bfloat16),
            pltpu.VMEM((rows // 2, width), jnp.bfloat16),
            pltpu.VMEM((2, rows, width), jnp.float32),
            pltpu.VMEM((2, rows, 1), jnp.float32),
            pltpu.VMEM((2, rows, 128), jnp.float32),
            pltpu.SemaphoreType.DMA((2,)),
            pltpu.SemaphoreType.DMA((4, ROUNDS)),
            pltpu.SemaphoreType.DMA((4, ROUNDS)),
        ],
        compiler_params=pltpu.CompilerParams(
            collective_id=0, has_side_effects=True, vmem_limit_bytes=48 * 1024 * 1024
        ),
    )(image_embed, text_embed, logit_scale, logit_bias)
    return loss[0], image_grad, text_grad


def solution(mesh):
    return jax.shard_map(
        functools.partial(local, mesh.shape["dp"]),
        mesh=mesh,
        in_specs=(P("dp", None), P("dp", None), P(), P()),
        out_specs=(P("dp"), P("dp", None), P("dp", None)),
        check_vma=False,
    )
```

```python
import functools

import jax
import jax.numpy as jnp
from jax import lax
from jax.experimental import pallas as pl
from jax.experimental.pallas import tpu as pltpu
from jax.sharding import PartitionSpec as P

MESH = pl.DeviceIdType.MESH
WINDOW = 5
EPS = 1e-06
TEXT, IMAGE = 0, 1
SHARED, RELAYED, DIRECT, SIBLING = range(4)
HELD = 256
MIB = 1024 * 1024


def pieces_of(rows):
    cuts = [(TEXT, 0, 256), (TEXT, 256, 256), (IMAGE, 0, 256), (IMAGE, 256, 128), (IMAGE, 384, 64), (IMAGE, 448, 64)]
    assert rows == 512
    return cuts


def inverse_length(rows):
    return lax.rsqrt(jnp.sum(rows * rows, axis=1, keepdims=True) + EPS)


def cosines(held, other):
    return lax.dot_general(held, other, (((1,), (1,)), ((), ())), preferred_element_type=jnp.float32)


def unit_gradient(summed, raw, factor):
    unit = raw.astype(jnp.float32) * factor
    along = jnp.sum(summed * unit, axis=1, keepdims=True)
    return (summed - unit * along) * factor


def exchange(n, img, txt, scale_ref, bias_ref,
             image_grad, text_total, text_unit, text_raw, text_factor, last, row_loss, params,
             image_total, image_unit, image_raw, image_factor, buf, chunk, loss_acc,
             load_sem, send_sem, recv_sem):
    rows = img.shape[0]
    pieces = pieces_of(rows)
    me = lax.axis_index("dp")
    core = lax.rem(me, 2)
    sibling = me + 1 - 2 * core
    step = 2 * core - 1
    ahead = lax.rem(me + 2 * step + n, n)
    behind = lax.rem(me - 2 * step + n, n)
    across = lax.rem(me + step + n, n)

    barrier = pltpu.get_barrier_semaphore()
    for other in (behind, across, sibling):
        pl.semaphore_signal(barrier, inc=1, device_id=(other,), device_id_type=MESH)
    loads = [
        pltpu.make_async_copy(source, target, load_sem.at[i])
        for i, (source, target) in enumerate(
            ((txt, text_raw), (img, image_raw))
        )
    ]
    for load in loads:
        load.start()
    pl.semaphore_wait(barrier, 3)

    def remote(source, way, piece, target):
        kind, first, size = pieces[piece]
        return pltpu.make_async_remote_copy(
            source, buf.at[way, kind, pl.ds(first, size)], send_sem.at[way, piece], recv_sem.at[way, piece],
            device_id=(target,), device_id_type=MESH,
        )

    def own_rows(piece):
        kind, first, size = pieces[piece]
        return (txt, img)[kind].at[pl.ds(first, size)]

    def landed(way, piece):
        kind, first, size = pieces[piece]
        return buf.at[way, kind, pl.ds(first, size)]

    everything = range(len(pieces))
    shared = [remote(own_rows(p), SHARED, p, ahead) for p in everything]
    direct = [remote(landed(SIBLING, p), DIRECT, p, across) for p in everything]
    beside = [remote(own_rows(p), SIBLING, p, sibling) for p in everything]
    relays = [remote(landed(SHARED, p), RELAYED, p, sibling) for p in everything]
    for copy in shared:
        copy.start()
    for copy in beside:
        copy.start()

    for load in loads:
        load.wait()
    scale = scale_ref[0]
    bias = bias_ref[0]
    params[0:8] = jnp.full((8, 128), scale, jnp.float32)
    params[8:16] = jnp.full((8, 128), bias, jnp.float32)

    for raw, unit, factor_ref in ((text_raw, text_unit, text_factor), (image_raw, image_unit, image_factor)):
        @pl.loop(0, rows // 128)
        def _(tile):
            span = pl.ds(pl.multiple_of(tile * 128, 128), 128)
            values = raw[span].astype(jnp.float32)
            factor = inverse_length(values)
            factor_ref[span] = factor
            unit[span] = (values * factor).astype(jnp.bfloat16)

    image_total[...] = jnp.zeros_like(image_total)
    text_total[...] = jnp.zeros_like(text_total)
    loss_acc[...] = jnp.zeros_like(loss_acc)

    def pairs(kind, other, size, offset=None):
        held_unit, total = ((image_unit, image_total), (text_unit, text_total))[kind]
        for tile in range(rows // HELD):
            held = pl.ds(tile * HELD, HELD)
            logits = scale * cosines(held_unit[held], other[...]) + bias
            grown = jnp.exp(logits)
            above = 1.0 + grown
            share = grown * pl.reciprocal(above)
            if offset is not None:
                row = lax.broadcasted_iota(jnp.int32, logits.shape, 0) + tile * HELD
                column = lax.broadcasted_iota(jnp.int32, logits.shape, 1)
                positive = row - column == offset
                share = share - jnp.where(positive, 1.0, 0.0)
            if kind == TEXT:
                small = grown * (1.0 - grown * (0.5 - grown * (1.0 / 3.0)))
                loss = jnp.where(grown < 0.0078125, small, jnp.log(above))
                if offset is not None:
                    loss = loss - jnp.where(positive, logits, 0.0)
                loss_acc[held] += functools.reduce(jnp.add, [loss[:, i:i + 128] for i in range(0, size, 128)])
            weights = (scale * share).astype(jnp.bfloat16)
            total[held] += jnp.dot(weights, other[...], preferred_element_type=jnp.float32)

    def unit_rows(source, target, size):
        step = min(size, 128)
        for first in range(0, size, step):
            values = source[first:first + step].astype(jnp.float32)
            target[first:first + step] = (values * inverse_length(values)).astype(jnp.bfloat16)

    def received(way, kind, first, size):
        unit_rows(buf.at[way, kind, pl.ds(first, size)], chunk, size)
        pairs(kind, chunk.at[pl.ds(0, size)], size)

    for kind, unit in ((TEXT, text_unit), (IMAGE, image_unit)):
        @pl.loop(0, rows // 256)
        def _(tile):
            first = pl.multiple_of(tile * 256, 256)
            pairs(kind, unit.at[pl.ds(first, 256)], 256, first)

    for copy in beside:
        copy.wait_recv()
    for kind in (TEXT, IMAGE):
        @pl.loop(0, rows // 256)
        def _(tile):
            received(SIBLING, kind, pl.multiple_of(tile * 256, 256), 256)

    for copy in direct:
        copy.start()

    def finish_images():
        @pl.loop(0, rows // 64)
        def _(tile):
            span = pl.ds(pl.multiple_of(tile * 64, 64), 64)
            image_grad[span] = unit_gradient(image_total[span], image_raw[span], image_factor[span])

        summed = lax.dot_general(
            jnp.full((8, 128), 1.0, jnp.float32), loss_acc[...], (((1,), (1,)), ((), ())),
            preferred_element_type=jnp.float32, precision=lax.Precision.HIGHEST,
        )
        row_loss[...] = summed[0:1] * (1.0 / (WINDOW * rows))

    def near(piece):
        shared[piece].wait_recv()
        relays[piece].start()
        received(SHARED, *pieces[piece])
        relays[piece].wait_recv()
        received(RELAYED, *pieces[piece])

    def far(piece):
        direct[piece].wait_recv()
        received(DIRECT, *pieces[piece])

    texts = [p for p in everything if pieces[p][0] == TEXT]
    images = [p for p in everything if pieces[p][0] == IMAGE]
    for piece in everything:
        near(piece)
    for piece in texts:
        far(piece)
    finish_images()
    for piece in images[:-1]:
        far(piece)
    direct[images[-1]].wait_recv()
    unit_rows(landed(DIRECT, images[-1]), last, last.shape[0])
    for copy in shared + direct + beside + relays:
        copy.wait_send()


def complete(image_done, text_total, text_unit, text_raw, text_factor, last, loss_done, params,
             row_loss, image_grad, text_grad, out, sem):
    rows = text_unit.shape[0]
    size = last.shape[0]
    tile = 128
    copies = [pltpu.make_async_copy(image_done, image_grad, sem.at[0]), pltpu.make_async_copy(loss_done, row_loss, sem.at[1])]
    for copy in copies:
        copy.start()
    scale = params[0:1, 0:size]
    bias = params[8:9, 0:size]
    for i in range(rows // tile):
        held = pl.ds(i * tile, tile)
        grown = jnp.exp(scale * cosines(text_unit[held], last[...]) + bias)
        weights = (scale * (grown * pl.reciprocal(1.0 + grown))).astype(jnp.bfloat16)
        summed = text_total[held] + jnp.dot(weights, last[...], preferred_element_type=jnp.float32)
        out[held] = unit_gradient(summed, text_raw[held], text_factor[held])
        copy = pltpu.make_async_copy(out.at[held], text_grad.at[held], sem.at[2 + i])
        copy.start()
        copies.append(copy)
    for copy in copies:
        copy.wait()


def local(n, image_embed, text_embed, logit_scale, logit_bias):
    rows, width = image_embed.shape
    pieces = pieces_of(rows)
    f32, bf16 = jnp.float32, jnp.bfloat16
    anywhere = pl.BlockSpec(memory_space=pl.ANY)
    hbm = pl.BlockSpec(memory_space=pltpu.HBM)
    vmem = pl.BlockSpec(memory_space=pltpu.VMEM)
    smem = pl.BlockSpec(memory_space=pltpu.SMEM)
    last_rows = pieces[-1][2]
    between = pl.pallas_call(
        functools.partial(exchange, n),
        out_shape=(
            pltpu.VMEM((rows, width), f32),
            pltpu.VMEM((rows, width), f32),
            pltpu.VMEM((rows, width), bf16),
            pltpu.VMEM((rows, width), bf16),
            pltpu.VMEM((rows, 1), f32),
            pltpu.VMEM((last_rows, width), bf16),
            pltpu.VMEM((1, rows), f32),
            pltpu.VMEM((16, 128), f32),
        ),
        in_specs=[hbm, hbm, smem, smem],
        out_specs=[vmem] * 8,
        scratch_shapes=[
            pltpu.VMEM((rows, width), f32),
            pltpu.VMEM((rows, width), bf16),
            pltpu.VMEM((rows, width), bf16),
            pltpu.VMEM((rows, 1), f32),
            pltpu.VMEM((4, 2, rows, width), bf16),
            pltpu.VMEM((256, width), bf16),
            pltpu.VMEM((rows, 128), f32),
            pltpu.SemaphoreType.DMA((2,)),
            pltpu.SemaphoreType.DMA((4, len(pieces))),
            pltpu.SemaphoreType.DMA((4, len(pieces))),
        ],
        compiler_params=pltpu.CompilerParams(collective_id=0, has_side_effects=True, vmem_limit_bytes=55 * MIB),
    )(image_embed, text_embed, logit_scale, logit_bias)
    row_loss, image_grad, text_grad = pl.pallas_call(
        complete,
        out_shape=(
            jax.ShapeDtypeStruct((1, rows), f32),
            jax.ShapeDtypeStruct((rows, width), f32),
            jax.ShapeDtypeStruct((rows, width), f32),
        ),
        in_specs=[vmem] * 8,
        out_specs=[anywhere] * 3,
        scratch_shapes=[pltpu.VMEM((rows, width), f32), pltpu.SemaphoreType.DMA((2 + rows // 128,))],
        compiler_params=pltpu.CompilerParams(vmem_limit_bytes=40 * MIB),
    )(*between)
    return row_loss[0], image_grad, text_grad


def solution(mesh):
    return jax.shard_map(
        functools.partial(local, mesh.shape["dp"]),
        mesh=mesh,
        in_specs=(P("dp", None), P("dp", None), P(), P()),
        out_specs=(P("dp"), P("dp", None), P("dp", None)),
        check_vma=False,
    )
```

```python
import functools

import jax
import jax.numpy as jnp
from jax import lax
from jax.experimental import pallas as pl
from jax.experimental.pallas import tpu as pltpu
from jax.sharding import PartitionSpec as P

MESH = pl.DeviceIdType.MESH
WINDOW = 5
EPS = 1e-06
TEXT, IMAGE = 0, 1
SHARED, RELAYED, DIRECT, SIBLING = range(4)
HELD = 256
MIB = 1024 * 1024


def pieces_of(rows):
    cuts = [(TEXT, 0, 256), (TEXT, 256, 256), (IMAGE, 0, 256), (IMAGE, 256, 128), (IMAGE, 384, 64), (IMAGE, 448, 64)]
    assert rows == 512
    return cuts


def inverse_length(rows):
    return lax.rsqrt(jnp.sum(rows * rows, axis=1, keepdims=True) + EPS)


def cosines(held, other):
    return lax.dot_general(held, other, (((1,), (1,)), ((), ())), preferred_element_type=jnp.float32)


def unit_gradient(summed, raw, factor):
    unit = raw.astype(jnp.float32) * factor
    along = jnp.sum(summed * unit, axis=1, keepdims=True)
    return (summed - unit * along) * factor


def exchange(n, img, txt, scale_ref, bias_ref,
             image_grad, text_total, text_unit, text_raw, text_factor, last, row_loss, params,
             image_total, image_unit, image_raw, image_factor, buf, chunk, loss_acc,
             load_sem, send_sem, recv_sem):
    rows = img.shape[0]
    pieces = pieces_of(rows)
    me = lax.axis_index("dp")
    core = lax.rem(me, 2)
    sibling = me + 1 - 2 * core
    step = 2 * core - 1
    ahead = lax.rem(me + 2 * step + n, n)
    behind = lax.rem(me - 2 * step + n, n)
    across = lax.rem(me + step + n, n)

    barrier = pltpu.get_barrier_semaphore()
    for other in (behind, across, sibling):
        pl.semaphore_signal(barrier, inc=1, device_id=(other,), device_id_type=MESH)
    loads = [
        pltpu.make_async_copy(source, target, load_sem.at[i])
        for i, (source, target) in enumerate(
            ((txt, text_raw), (img, image_raw))
        )
    ]
    for load in loads:
        load.start()
    pl.semaphore_wait(barrier, 3)

    def remote(source, way, piece, target):
        kind, first, size = pieces[piece]
        return pltpu.make_async_remote_copy(
            source, buf.at[way, kind, pl.ds(first, size)], send_sem.at[way, piece], recv_sem.at[way, piece],
            device_id=(target,), device_id_type=MESH,
        )

    def own_rows(piece):
        kind, first, size = pieces[piece]
        return (txt, img)[kind].at[pl.ds(first, size)]

    def landed(way, piece):
        kind, first, size = pieces[piece]
        return buf.at[way, kind, pl.ds(first, size)]

    everything = range(len(pieces))
    shared = [remote(own_rows(p), SHARED, p, ahead) for p in everything]
    direct = [remote(landed(SIBLING, p), DIRECT, p, across) for p in everything]
    beside = [remote(own_rows(p), SIBLING, p, sibling) for p in everything]
    relays = [remote(landed(SHARED, p), RELAYED, p, sibling) for p in everything]
    for copy in shared:
        copy.start()
    for copy in beside:
        copy.start()

    for load in loads:
        load.wait()
    scale = scale_ref[0]
    bias = bias_ref[0]
    params[0:8] = jnp.full((8, 128), scale, jnp.float32)
    params[8:16] = jnp.full((8, 128), bias, jnp.float32)

    for raw, unit, factor_ref in ((text_raw, text_unit, text_factor), (image_raw, image_unit, image_factor)):
        @pl.loop(0, rows // 128)
        def _(tile):
            span = pl.ds(pl.multiple_of(tile * 128, 128), 128)
            values = raw[span].astype(jnp.float32)
            factor = inverse_length(values)
            factor_ref[span] = factor
            unit[span] = (values * factor).astype(jnp.bfloat16)

    image_total[...] = jnp.zeros_like(image_total)
    text_total[...] = jnp.zeros_like(text_total)
    loss_acc[...] = jnp.zeros_like(loss_acc)

    def pairs(kind, other, size, offset=None):
        held_unit, total = ((image_unit, image_total), (text_unit, text_total))[kind]
        for tile in range(rows // HELD):
            held = pl.ds(tile * HELD, HELD)
            logits = scale * cosines(held_unit[held], other[...]) + bias
            grown = jnp.exp(logits)
            above = 1.0 + grown
            share = grown * pl.reciprocal(above)
            if offset is not None:
                row = lax.broadcasted_iota(jnp.int32, logits.shape, 0) + tile * HELD
                column = lax.broadcasted_iota(jnp.int32, logits.shape, 1)
                positive = row - column == offset
                share = share - jnp.where(positive, 1.0, 0.0)
            if kind == TEXT:
                small = grown * (1.0 - grown * (0.5 - grown * (1.0 / 3.0)))
                loss = jnp.where(grown < 0.0078125, small, jnp.log(above))
                if offset is not None:
                    loss = loss - jnp.where(positive, logits, 0.0)
                loss_acc[held] += functools.reduce(jnp.add, [loss[:, i:i + 128] for i in range(0, size, 128)])
            weights = (scale * share).astype(jnp.bfloat16)
            total[held] += jnp.dot(weights, other[...], preferred_element_type=jnp.float32)

    def unit_rows(source, target, size):
        step = min(size, 128)
        for first in range(0, size, step):
            values = source[first:first + step].astype(jnp.float32)
            target[first:first + step] = (values * inverse_length(values)).astype(jnp.bfloat16)

    def received(way, kind, first, size):
        unit_rows(buf.at[way, kind, pl.ds(first, size)], chunk, size)
        pairs(kind, chunk.at[pl.ds(0, size)], size)

    for kind, unit in ((TEXT, text_unit), (IMAGE, image_unit)):
        @pl.loop(0, rows // 256)
        def _(tile):
            first = pl.multiple_of(tile * 256, 256)
            pairs(kind, unit.at[pl.ds(first, 256)], 256, first)

    for copy in beside:
        copy.wait_recv()
    for copy in direct:
        copy.start()

    for kind in (TEXT, IMAGE):
        @pl.loop(0, rows // 256)
        def _(tile):
            received(SIBLING, kind, pl.multiple_of(tile * 256, 256), 256)

    def finish_images():
        @pl.loop(0, rows // 64)
        def _(tile):
            span = pl.ds(pl.multiple_of(tile * 64, 64), 64)
            image_grad[span] = unit_gradient(image_total[span], image_raw[span], image_factor[span])

        summed = lax.dot_general(
            jnp.full((8, 128), 1.0, jnp.float32), loss_acc[...], (((1,), (1,)), ((), ())),
            preferred_element_type=jnp.float32, precision=lax.Precision.HIGHEST,
        )
        row_loss[...] = summed[0:1] * (1.0 / (WINDOW * rows))

    def near(piece):
        shared[piece].wait_recv()
        relays[piece].start()
        received(SHARED, *pieces[piece])
        relays[piece].wait_recv()
        received(RELAYED, *pieces[piece])

    def far(piece):
        direct[piece].wait_recv()
        received(DIRECT, *pieces[piece])

    texts = [p for p in everything if pieces[p][0] == TEXT]
    images = [p for p in everything if pieces[p][0] == IMAGE]
    for piece in everything:
        near(piece)
    for piece in texts:
        far(piece)
    finish_images()
    for piece in images[:-1]:
        far(piece)
    direct[images[-1]].wait_recv()
    unit_rows(landed(DIRECT, images[-1]), last, last.shape[0])
    for copy in shared + direct + beside + relays:
        copy.wait_send()


def complete(image_done, text_total, text_unit, text_raw, text_factor, last, loss_done, params,
             row_loss, image_grad, text_grad, out, sem):
    rows = text_unit.shape[0]
    size = last.shape[0]
    tile = 128
    copies = [pltpu.make_async_copy(image_done, image_grad, sem.at[0]), pltpu.make_async_copy(loss_done, row_loss, sem.at[1])]
    for copy in copies:
        copy.start()
    scale = params[0:1, 0:size]
    bias = params[8:9, 0:size]
    for i in range(rows // tile):
        held = pl.ds(i * tile, tile)
        grown = jnp.exp(scale * cosines(text_unit[held], last[...]) + bias)
        weights = (scale * (grown * pl.reciprocal(1.0 + grown))).astype(jnp.bfloat16)
        summed = text_total[held] + jnp.dot(weights, last[...], preferred_element_type=jnp.float32)
        out[held] = unit_gradient(summed, text_raw[held], text_factor[held])
        copy = pltpu.make_async_copy(out.at[held], text_grad.at[held], sem.at[2 + i])
        copy.start()
        copies.append(copy)
    for copy in copies:
        copy.wait()


def local(n, image_embed, text_embed, logit_scale, logit_bias):
    rows, width = image_embed.shape
    pieces = pieces_of(rows)
    f32, bf16 = jnp.float32, jnp.bfloat16
    anywhere = pl.BlockSpec(memory_space=pl.ANY)
    hbm = pl.BlockSpec(memory_space=pltpu.HBM)
    vmem = pl.BlockSpec(memory_space=pltpu.VMEM)
    smem = pl.BlockSpec(memory_space=pltpu.SMEM)
    last_rows = pieces[-1][2]
    between = pl.pallas_call(
        functools.partial(exchange, n),
        out_shape=(
            pltpu.VMEM((rows, width), f32),
            pltpu.VMEM((rows, width), f32),
            pltpu.VMEM((rows, width), bf16),
            pltpu.VMEM((rows, width), bf16),
            pltpu.VMEM((rows, 1), f32),
            pltpu.VMEM((last_rows, width), bf16),
            pltpu.VMEM((1, rows), f32),
            pltpu.VMEM((16, 128), f32),
        ),
        in_specs=[hbm, hbm, smem, smem],
        out_specs=[vmem] * 8,
        scratch_shapes=[
            pltpu.VMEM((rows, width), f32),
            pltpu.VMEM((rows, width), bf16),
            pltpu.VMEM((rows, width), bf16),
            pltpu.VMEM((rows, 1), f32),
            pltpu.VMEM((4, 2, rows, width), bf16),
            pltpu.VMEM((256, width), bf16),
            pltpu.VMEM((rows, 128), f32),
            pltpu.SemaphoreType.DMA((2,)),
            pltpu.SemaphoreType.DMA((4, len(pieces))),
            pltpu.SemaphoreType.DMA((4, len(pieces))),
        ],
        compiler_params=pltpu.CompilerParams(collective_id=0, has_side_effects=True, vmem_limit_bytes=55 * MIB),
    )(image_embed, text_embed, logit_scale, logit_bias)
    row_loss, image_grad, text_grad = pl.pallas_call(
        complete,
        out_shape=(
            jax.ShapeDtypeStruct((1, rows), f32),
            jax.ShapeDtypeStruct((rows, width), f32),
            jax.ShapeDtypeStruct((rows, width), f32),
        ),
        in_specs=[vmem] * 8,
        out_specs=[anywhere] * 3,
        scratch_shapes=[pltpu.VMEM((rows, width), f32), pltpu.SemaphoreType.DMA((2 + rows // 128,))],
        compiler_params=pltpu.CompilerParams(vmem_limit_bytes=40 * MIB),
    )(*between)
    return row_loss[0], image_grad, text_grad


def solution(mesh):
    return jax.shard_map(
        functools.partial(local, mesh.shape["dp"]),
        mesh=mesh,
        in_specs=(P("dp", None), P("dp", None), P(), P()),
        out_specs=(P("dp"), P("dp", None), P("dp", None)),
        check_vma=False,
    )
```

```python
import functools

import jax
import jax.numpy as jnp
from jax import lax
from jax.experimental import pallas as pl
from jax.experimental.pallas import tpu as pltpu
from jax.sharding import PartitionSpec as P

MESH = pl.DeviceIdType.MESH
WINDOW = 5
EPS = 1e-06
TEXT, IMAGE = 0, 1
SHARED, RELAYED, DIRECT, SIBLING = range(4)
HELD = 256
MIB = 1024 * 1024


def pieces_of(rows):
    cuts = [(TEXT, 0, 256), (TEXT, 256, 256), (IMAGE, 0, 256), (IMAGE, 256, 192), (IMAGE, 448, 64)]
    assert rows == 512
    return cuts


def inverse_length(rows):
    return lax.rsqrt(jnp.sum(rows * rows, axis=1, keepdims=True) + EPS)


def cosines(held, other):
    return lax.dot_general(held, other, (((1,), (1,)), ((), ())), preferred_element_type=jnp.float32)


def unit_gradient(summed, raw, factor):
    unit = raw.astype(jnp.float32) * factor
    along = jnp.sum(summed * unit, axis=1, keepdims=True)
    return (summed - unit * along) * factor


def exchange(n, img, txt, scale_ref, bias_ref,
             image_grad, text_total, text_unit, text_raw, text_factor, last, row_loss, params,
             image_total, image_unit, image_raw, image_factor, buf, chunk, loss_acc,
             load_sem, send_sem, recv_sem):
    rows = img.shape[0]
    pieces = pieces_of(rows)
    me = lax.axis_index("dp")
    core = lax.rem(me, 2)
    sibling = me + 1 - 2 * core
    step = 2 * core - 1
    ahead = lax.rem(me + 2 * step + n, n)
    behind = lax.rem(me - 2 * step + n, n)
    across = lax.rem(me + step + n, n)

    barrier = pltpu.get_barrier_semaphore()
    for other in (across, behind, sibling):
        pl.semaphore_signal(barrier, inc=1, device_id=(other,), device_id_type=MESH)
    loads = [
        pltpu.make_async_copy(source, target, load_sem.at[i])
        for i, (source, target) in enumerate(
            ((txt, text_raw), (img, image_raw))
        )
    ]
    for load in loads:
        load.start()
    pl.semaphore_wait(barrier, 3)

    def remote(source, way, piece, target):
        kind, first, size = pieces[piece]
        return pltpu.make_async_remote_copy(
            source, buf.at[way, kind, pl.ds(first, size)], send_sem.at[way, piece], recv_sem.at[way, piece],
            device_id=(target,), device_id_type=MESH,
        )

    def own_rows(piece):
        kind, first, size = pieces[piece]
        return (txt, img)[kind].at[pl.ds(first, size)]

    def landed(way, piece):
        kind, first, size = pieces[piece]
        return buf.at[way, kind, pl.ds(first, size)]

    everything = range(len(pieces))
    shared = [remote(own_rows(p), SHARED, p, ahead) for p in everything]
    direct = [remote(landed(SIBLING, p), DIRECT, p, across) for p in everything]
    beside = [remote(own_rows(p), SIBLING, p, sibling) for p in everything]
    relays = [remote(landed(SHARED, p), RELAYED, p, sibling) for p in everything]
    for copy in shared:
        copy.start()
    for copy in beside:
        copy.start()

    for load in loads:
        load.wait()
    scale = scale_ref[0]
    bias = bias_ref[0]
    params[0:8] = jnp.full((8, 128), scale, jnp.float32)
    params[8:16] = jnp.full((8, 128), bias, jnp.float32)

    for raw, unit, factor_ref in ((text_raw, text_unit, text_factor), (image_raw, image_unit, image_factor)):
        @pl.loop(0, rows // 128)
        def _(tile):
            span = pl.ds(pl.multiple_of(tile * 128, 128), 128)
            values = raw[span].astype(jnp.float32)
            factor = inverse_length(values)
            factor_ref[span] = factor
            unit[span] = (values * factor).astype(jnp.bfloat16)

    image_total[...] = jnp.zeros_like(image_total)
    text_total[...] = jnp.zeros_like(text_total)
    loss_acc[...] = jnp.zeros_like(loss_acc)

    def pairs(kind, other, size, offset=None):
        held_unit, total = ((image_unit, image_total), (text_unit, text_total))[kind]
        for tile in range(rows // HELD):
            held = pl.ds(tile * HELD, HELD)
            logits = scale * cosines(held_unit[held], other[...]) + bias
            grown = jnp.exp(logits)
            above = 1.0 + grown
            share = grown * pl.reciprocal(above)
            if offset is not None:
                row = lax.broadcasted_iota(jnp.int32, logits.shape, 0) + tile * HELD
                column = lax.broadcasted_iota(jnp.int32, logits.shape, 1)
                positive = row - column == offset
                share = share - jnp.where(positive, 1.0, 0.0)
            if kind == TEXT:
                small = grown * (1.0 - grown * (0.5 - grown * (1.0 / 3.0)))
                loss = jnp.where(grown < 0.0078125, small, jnp.log(above))
                if offset is not None:
                    loss = loss - jnp.where(positive, logits, 0.0)
                loss_acc[held] += functools.reduce(jnp.add, [loss[:, i:i + 128] for i in range(0, size, 128)])
            weights = (scale * share).astype(jnp.bfloat16)
            total[held] += jnp.dot(weights, other[...], preferred_element_type=jnp.float32)

    def unit_rows(source, target, size):
        step = 128 if size % 128 == 0 else 64
        for first in range(0, size, step):
            values = source[first:first + step].astype(jnp.float32)
            target[first:first + step] = (values * inverse_length(values)).astype(jnp.bfloat16)

    def received(way, kind, first, size):
        unit_rows(buf.at[way, kind, pl.ds(first, size)], chunk, size)
        pairs(kind, chunk.at[pl.ds(0, size)], size)

    for kind, unit in ((TEXT, text_unit), (IMAGE, image_unit)):
        @pl.loop(0, rows // 256)
        def _(tile):
            first = pl.multiple_of(tile * 256, 256)
            pairs(kind, unit.at[pl.ds(first, 256)], 256, first)

    for copy in beside:
        copy.wait_recv()
    for copy in direct:
        copy.start()

    for kind in (TEXT, IMAGE):
        @pl.loop(0, rows // 256)
        def _(tile):
            received(SIBLING, kind, pl.multiple_of(tile * 256, 256), 256)

    def finish_images():
        @pl.loop(0, rows // 64)
        def _(tile):
            span = pl.ds(pl.multiple_of(tile * 64, 64), 64)
            image_grad[span] = unit_gradient(image_total[span], image_raw[span], image_factor[span])

        summed = lax.dot_general(
            jnp.full((8, 128), 1.0, jnp.float32), loss_acc[...], (((1,), (1,)), ((), ())),
            preferred_element_type=jnp.float32, precision=lax.Precision.HIGHEST,
        )
        row_loss[...] = summed[0:1] * (1.0 / (WINDOW * rows))

    def near(piece):
        shared[piece].wait_recv()
        relays[piece].start()
        received(SHARED, *pieces[piece])
        relays[piece].wait_recv()
        received(RELAYED, *pieces[piece])

    def far(piece):
        direct[piece].wait_recv()
        received(DIRECT, *pieces[piece])

    texts = [p for p in everything if pieces[p][0] == TEXT]
    images = [p for p in everything if pieces[p][0] == IMAGE]
    for piece in everything:
        near(piece)
    for piece in texts:
        far(piece)
    finish_images()
    for piece in images[:-1]:
        far(piece)
    direct[images[-1]].wait_recv()
    unit_rows(landed(DIRECT, images[-1]), last, last.shape[0])
    for copy in shared + direct + beside + relays:
        copy.wait_send()


def complete(image_done, text_total, text_unit, text_raw, text_factor, last, loss_done, params,
             row_loss, image_grad, text_grad, out, sem):
    rows = text_unit.shape[0]
    size = last.shape[0]
    tile = 128
    copies = [pltpu.make_async_copy(image_done, image_grad, sem.at[0]), pltpu.make_async_copy(loss_done, row_loss, sem.at[1])]
    for copy in copies:
        copy.start()
    scale = params[0:1, 0:size]
    bias = params[8:9, 0:size]
    for i in range(rows // tile):
        held = pl.ds(i * tile, tile)
        grown = jnp.exp(scale * cosines(text_unit[held], last[...]) + bias)
        weights = (scale * (grown * pl.reciprocal(1.0 + grown))).astype(jnp.bfloat16)
        summed = text_total[held] + jnp.dot(weights, last[...], preferred_element_type=jnp.float32)
        out[held] = unit_gradient(summed, text_raw[held], text_factor[held])
        copy = pltpu.make_async_copy(out.at[held], text_grad.at[held], sem.at[2 + i])
        copy.start()
        copies.append(copy)
    for copy in copies:
        copy.wait()


def local(n, image_embed, text_embed, logit_scale, logit_bias):
    rows, width = image_embed.shape
    pieces = pieces_of(rows)
    f32, bf16 = jnp.float32, jnp.bfloat16
    anywhere = pl.BlockSpec(memory_space=pl.ANY)
    hbm = pl.BlockSpec(memory_space=pltpu.HBM)
    vmem = pl.BlockSpec(memory_space=pltpu.VMEM)
    smem = pl.BlockSpec(memory_space=pltpu.SMEM)
    last_rows = pieces[-1][2]
    between = pl.pallas_call(
        functools.partial(exchange, n),
        out_shape=(
            pltpu.VMEM((rows, width), f32),
            pltpu.VMEM((rows, width), f32),
            pltpu.VMEM((rows, width), bf16),
            pltpu.VMEM((rows, width), bf16),
            pltpu.VMEM((rows, 1), f32),
            pltpu.VMEM((last_rows, width), bf16),
            pltpu.VMEM((1, rows), f32),
            pltpu.VMEM((16, 128), f32),
        ),
        in_specs=[hbm, hbm, smem, smem],
        out_specs=[vmem] * 8,
        scratch_shapes=[
            pltpu.VMEM((rows, width), f32),
            pltpu.VMEM((rows, width), bf16),
            pltpu.VMEM((rows, width), bf16),
            pltpu.VMEM((rows, 1), f32),
            pltpu.VMEM((4, 2, rows, width), bf16),
            pltpu.VMEM((256, width), bf16),
            pltpu.VMEM((rows, 128), f32),
            pltpu.SemaphoreType.DMA((2,)),
            pltpu.SemaphoreType.DMA((4, len(pieces))),
            pltpu.SemaphoreType.DMA((4, len(pieces))),
        ],
        compiler_params=pltpu.CompilerParams(collective_id=0, has_side_effects=True, vmem_limit_bytes=55 * MIB),
    )(image_embed, text_embed, logit_scale, logit_bias)
    row_loss, image_grad, text_grad = pl.pallas_call(
        complete,
        out_shape=(
            jax.ShapeDtypeStruct((1, rows), f32),
            jax.ShapeDtypeStruct((rows, width), f32),
            jax.ShapeDtypeStruct((rows, width), f32),
        ),
        in_specs=[vmem] * 8,
        out_specs=[anywhere] * 3,
        scratch_shapes=[pltpu.VMEM((rows, width), f32), pltpu.SemaphoreType.DMA((2 + rows // 128,))],
        compiler_params=pltpu.CompilerParams(vmem_limit_bytes=40 * MIB),
    )(*between)
    return row_loss[0], image_grad, text_grad


def solution(mesh):
    return jax.shard_map(
        functools.partial(local, mesh.shape["dp"]),
        mesh=mesh,
        in_specs=(P("dp", None), P("dp", None), P(), P()),
        out_specs=(P("dp"), P("dp", None), P("dp", None)),
        check_vma=False,
    )
```
